32 devices in a mesh: blk: 16 (over z, x, core), rep: 2 (over y).
Axes of the slice: x: 2, y: 2, z: 4, core: 2. Of those that a mesh axis runs over, the one named last changes fastest.
Arguments:
- features: bfloat16 [4096, 128], P('blk'), may hold values from -6 to 6
- tile_values: bfloat16 [16, 16, 16, 128, 128], P('blk', 'rep'), may hold values from -0.09375 to 0.09375
- tile_target: int32 [16, 16, 16], P('blk', 'rep'), may hold values from 0 to 1
- tile_source: int32 [16, 16, 16], P('blk', 'rep'), may hold values from 0 to 1
- tile_count: int32 [16, 16], P('blk', 'rep'), may hold values from 0 to 16, as said below
- hub_list: int32 [16, 16, 16], P('blk'), may hold values from 0 to 255
- hub_count: int32 [16, 16], P('blk'), may hold values from 0 to 16, as said below
- hub_weight: bfloat16 [16, 16, 4096], P(None, None, 'blk'), may hold values from -0.375 to 0.375
- self_weight: bfloat16 [128, 256], P(None, 'rep'), may hold values from -0.5 to 0.5
- neighbor_weight: bfloat16 [128, 256], P(None, 'rep'), may hold values from -0.5 to 0.5
- bias: float32 [256], P('rep'), may hold values from -3 to 3
- cotangent: bfloat16 [4096, 256], P('blk', 'rep'), may hold values from -6 to 6
Outputs:
- output: bfloat16 [4096, 256], P('blk', 'rep')
- grad_input: bfloat16 [4096, 128], P('blk')
- grad_self: float32 [128, 256], P(None, 'rep')
- grad_neighbor: float32 [128, 256], P(None, 'rep')
- grad_bias: float32 [256], P('rep')
The draws below stay inside these ranges and needn't reach their ends.
Inputs may be any that keep to these rules, and one draw needn't show every extreme that they name: Slots at or beyond tile_count of a pair of blocks carry values that no output reads. Offset 0 of every destination block has all 16 slots live; some destination blocks may have many slots live at every offset. Coordinates may repeat within a pair; their terms add. `hub_list`: entries may repeat within one list; slots at or beyond hub_count are unused. `hub_count`: every sending block s uses all 16 slots for the reading block (s + 1) mod 16.
All inputs are finite; a program needn't handle non-finite values.
Results may differ from the reference program's by a relative error of at most 0.0056.
Values may be sent and summed in bfloat16 or wider, within the bound.
A program may use at most 64 MiB of HBM per device.

```python
import math
import jax
import jax.numpy as jnp
from jax import lax

ROWS_DEV = 256
F = 128
HID = 256
TILE = 128
SLOTS = 16
HUB_MOST = 16
BLOCKS = 16
NODES = 4096
TILE_ROWS = 2


def draw_tile_count(key, part):
    heavy_rows = jax.random.randint(jax.random.fold_in(key, 11), (BLOCKS, 1), 0, 8) == 0
    base_counts = jax.random.randint(jax.random.fold_in(key, 12), (BLOCKS, BLOCKS), 0, 5)
    heavy_counts = jax.random.randint(jax.random.fold_in(key, 13), (BLOCKS, BLOCKS), SLOTS // 2, SLOTS + 1)
    counts = jnp.where(heavy_rows, heavy_counts, jnp.minimum(base_counts, SLOTS))
    counts = counts.at[:, 0].set(SLOTS)
    return counts.astype(jnp.int32)


def draw_hub_count(key, part):
    counts = jax.random.randint(jax.random.fold_in(key, 21), (BLOCKS, BLOCKS), 0, HUB_MOST + 1)
    next_reader = (jnp.arange(BLOCKS)[:, None] + 1) % BLOCKS == jnp.arange(BLOCKS)[None, :]
    return jnp.where(next_reader, HUB_MOST, counts).astype(jnp.int32)


def place_ends(drawn, own_key, smallest, largest):
    index_at = [jax.random.randint(jax.random.fold_in(own_key, axis), (), 0, length) for axis, length in enumerate(drawn.shape)]
    main_axis = drawn.shape.index(max(drawn.shape))
    neighbour = index_at[:main_axis] + [(index_at[main_axis] + 1) % drawn.shape[main_axis]] + index_at[main_axis + 1:]
    return drawn.at[tuple(index_at)].set(smallest).at[tuple(neighbour)].set(largest)


def block_levels(stream_key, shape, pieces, low, largest):
    loudness = 1.0
    for position, shards_of in pieces:
        steps = jax.random.uniform(jax.random.fold_in(jax.random.fold_in(stream_key, 6), position), (shards_of,), jnp.float32, low / len(pieces), largest / len(pieces))
        loudness = loudness * jnp.repeat(jnp.exp(steps), shape[position] // shards_of).reshape((-1,) + (1,) * (len(shape) - 1 - position))
    return loudness


def scatter_about(stream_key, extent, scale, reach, split=(), kind=jnp.bfloat16):
    loudness = block_levels(stream_key, extent, split, -0.22, 0.18) if split else 1.0
    entries = jax.random.normal(stream_key, extent, jnp.float32) * scale * loudness
    return jnp.minimum(jnp.maximum(entries, -reach), reach).astype(kind)


def setup_inputs(seed: int = 0) -> dict:
    key_of = jax.random.split(jax.random.key(seed), 13)
    return {
        "features": scatter_about(key_of[0], (NODES, F), 1.0, 6.0, ((0, 16),)),
        "tile_values": scatter_about(key_of[1], (BLOCKS, BLOCKS, SLOTS, TILE, TILE), (BLOCKS * 4 * TILE // TILE_ROWS) ** -0.5, 0.09375, ((0, 16), (1, 2))),
        "tile_target": place_ends(jax.random.randint(key_of[2], (BLOCKS, BLOCKS, SLOTS), 0, TILE_ROWS), jax.random.fold_in(key_of[2], 1), 0, TILE_ROWS - 1).astype(jnp.int32),
        "tile_source": place_ends(jax.random.randint(key_of[3], (BLOCKS, BLOCKS, SLOTS), 0, TILE_ROWS), jax.random.fold_in(key_of[3], 1), 0, TILE_ROWS - 1).astype(jnp.int32),
        "tile_count": draw_tile_count(jax.random.fold_in(key_of[12], 71), 0),
        "hub_list": place_ends(jax.random.randint(key_of[5], (BLOCKS, BLOCKS, HUB_MOST), 0, ROWS_DEV), jax.random.fold_in(key_of[5], 1), 0, ROWS_DEV - 1).astype(jnp.int32),
        "hub_count": draw_hub_count(jax.random.fold_in(key_of[12], 71), 0),
        "hub_weight": scatter_about(key_of[7], (BLOCKS, HUB_MOST, NODES), (BLOCKS * HUB_MOST) ** -0.5, 0.375, ((2, 16),)),
        "self_weight": scatter_about(key_of[8], (F, HID), F ** -0.5, 0.5, ((1, 2),)),
        "neighbor_weight": scatter_about(key_of[9], (F, HID), F ** -0.5, 0.5, ((1, 2),)),
        "bias": scatter_about(key_of[10], (HID,), 0.5, 3.0, ((0, 2),), jnp.float32),
        "cotangent": scatter_about(key_of[11], (NODES, HID), 1.0, 6.0, ((0, 16), (1, 2))),
    }


def reference(features, tile_values, tile_target, tile_source, tile_count, hub_list, hub_count, hub_weight, self_weight, neighbor_weight, bias, cotangent):
    blocks = tile_count.shape[0]
    node_count, feature_width = features.shape
    rows_dev = node_count // blocks
    tile_size = tile_values.shape[-1]
    tile_rows = rows_dev // tile_size
    slot_ids = jnp.arange(tile_values.shape[2], dtype=jnp.int32)
    hub_ids = jnp.arange(hub_list.shape[2], dtype=jnp.int32)
    sender_base = (jnp.arange(blocks, dtype=jnp.int32) * rows_dev)[:, None]
    feature_tiles = features.reshape(blocks, tile_rows, tile_size, feature_width)
    highest = lax.Precision.HIGHEST

    def block_terms(target, offset):
        source = (target - offset) % blocks
        active = (slot_ids < tile_count[target, offset]).astype(jnp.float32)
        return (source, tile_values[target, offset].astype(jnp.float32), active)

    def hub_terms(target):
        start = (target * rows_dev).astype(jnp.int32)
        weights = lax.dynamic_slice_in_dim(hub_weight, start, rows_dev, 2).astype(jnp.float32)
        hub_active = hub_ids[None, :] < hub_count[:, target][:, None]
        hub_rows = (sender_base + hub_list[:, target, :]).astype(jnp.int32)
        return (weights, hub_active, hub_rows)

    def aggregate_block(target):

        def one_offset(offset, totals):
            source, tile_block, active = block_terms(target, offset)
            picked = feature_tiles[source][tile_source[target, offset]].astype(jnp.float32)
            products = jnp.einsum('jab,jbf->jaf', tile_block, picked, precision=highest)
            placer = jax.nn.one_hot(tile_target[target, offset], tile_rows, dtype=jnp.float32) * active[:, None]
            return totals + jnp.einsum('jt,jaf->taf', placer, products, precision=highest)
        totals = lax.fori_loop(0, blocks, one_offset, jnp.zeros((tile_rows, tile_size, feature_width), jnp.float32))
        weights, hub_active, hub_rows = hub_terms(target)
        picked_rows = features[hub_rows].astype(jnp.float32)
        picked_rows = jnp.where(hub_active[:, :, None], picked_rows, jnp.zeros((), jnp.float32))
        hub_part = jnp.einsum('sjn,sjf->nf', weights, picked_rows, precision=highest)
        return totals.reshape(rows_dev, feature_width) + hub_part
    neighborhood = lax.map(aggregate_block, jnp.arange(blocks, dtype=jnp.int32))
    aggregate = neighborhood.reshape(node_count, feature_width).astype(jnp.bfloat16)
    pre_activation = jnp.dot(features, self_weight, preferred_element_type=jnp.float32) + jnp.dot(aggregate, neighbor_weight, preferred_element_type=jnp.float32) + bias
    output = jax.nn.silu(pre_activation).astype(jnp.bfloat16)
    gate_value = jax.nn.sigmoid(pre_activation)
    grad_activation = (cotangent.astype(jnp.float32) * gate_value * (1.0 + pre_activation * (1.0 - gate_value))).astype(jnp.bfloat16)
    grad_scale = 1.0 / math.sqrt(node_count)
    grad_self = jnp.dot(features.T, grad_activation, preferred_element_type=jnp.float32) * grad_scale
    grad_neighbor = jnp.dot(aggregate.T, grad_activation, preferred_element_type=jnp.float32) * grad_scale
    grad_bias = lax.optimization_barrier(jnp.sum(grad_activation.astype(jnp.float32), axis=0)) * grad_scale
    grad_aggregate = jnp.dot(grad_activation, neighbor_weight.T, preferred_element_type=jnp.float32).astype(jnp.bfloat16)
    self_grad = jnp.dot(grad_activation, self_weight.T, preferred_element_type=jnp.float32)
    grad_tiles = grad_aggregate.reshape(blocks, tile_rows, tile_size, feature_width)

    def spread_block(target, totals):

        def one_offset(offset, inner):
            source, tile_block, active = block_terms(target, offset)
            picked = grad_tiles[target][tile_target[target, offset]].astype(jnp.float32)
            products = jnp.einsum('jab,jaf->jbf', tile_block, picked, precision=highest)
            placer = jax.nn.one_hot(tile_source[target, offset], tile_rows, dtype=jnp.float32) * active[:, None]
            return inner.at[source].add(jnp.einsum('jt,jbf->tbf', placer, products, precision=highest))
        totals = lax.fori_loop(0, blocks, one_offset, totals)
        weights, hub_active, hub_rows = hub_terms(target)
        start = (target * rows_dev).astype(jnp.int32)
        reader_grad = lax.dynamic_slice_in_dim(grad_aggregate, start, rows_dev, 0).astype(jnp.float32)
        returned = jnp.einsum('sjn,nf->sjf', weights, reader_grad, precision=highest)
        returned = jnp.where(hub_active[:, :, None], returned, jnp.zeros((), jnp.float32))
        flat_grads = totals.reshape(node_count, feature_width).at[hub_rows.reshape(-1)].add(returned.reshape(-1, feature_width))
        return flat_grads.reshape(totals.shape)
    spread = lax.fori_loop(0, blocks, spread_block, jnp.zeros((blocks, tile_rows, tile_size, feature_width), jnp.float32))
    grad_input = (spread.reshape(node_count, feature_width) + self_grad).astype(jnp.bfloat16)
    return (output, grad_input, grad_self, grad_neighbor, grad_bias)
```

```python
import functools
import math

import jax
import jax.numpy as jnp
from jax import lax
from jax.experimental import pallas as pl
from jax.experimental.pallas import tpu as pltpu
from jax.sharding import PartitionSpec as P

MESH = pl.DeviceIdType.MESH
F32 = jnp.float32
BF16 = jnp.bfloat16


def mm(a, b, ca=1, cb=0):
    return lax.dot_general(a, b, (((ca,), (cb,)), ((), ())), preferred_element_type=F32)


def remote(src, dst, send, recv, device):
    return pltpu.make_async_remote_copy(
        src_ref=src, dst_ref=dst, send_sem=send, recv_sem=recv, device_id=device, device_id_type=MESH
    )


def kernel(
    blocks, grad_scale,
    features, tile_values, tile_target, tile_source, tile_count, hub_list, hub_count, hub_weight,
    self_weight, neighbor_weight, bias, cotangent,
    output, grad_input, grad_self, grad_neighbor, grad_bias,
    tiles, dense, xsend, xbuf, pick, rows_all, weight_all, total, codes,
    part_send, part_recv, back_send, back_recv, last_send, last_recv,
    aggregate, grad_act, pair_send, pair_recv, src_send, src_recv,
    w_send, w_recv, w_sum, w_out,
    tile_sem, xs, xr, fs, rep_s, rep_r, ps, pr, cs, cr, w1s, w1r, w2s, w2r,
):
    half = tile_values.shape[0]
    slots = tile_values.shape[1]
    tile = tile_values.shape[2]
    rows = features.shape[0]
    width = features.shape[1]
    hubs = hub_list.shape[1]
    chips = blocks // 2
    reach = half // 2
    me = lax.axis_index("blk")
    r = lax.axis_index("rep")
    k = me // 2
    c = me % 2
    partner = {"blk": k * 2 + 1 - c}
    other_rep = {"rep": 1 - r}

    for o in range(half):
        pltpu.make_async_copy(tile_values.at[o], tiles.at[o], tile_sem.at[o]).start()
    barrier = pltpu.get_barrier_semaphore()

    def greet(i, carry):
        pl.semaphore_signal(
            barrier, inc=1, device_id={"blk": (me + i) % blocks}, device_id_type=MESH
        )
        return carry

    lax.fori_loop(1, blocks, greet, 0)
    pl.semaphore_signal(barrier, inc=1, device_id=other_rep, device_id_type=MESH)

    xsend[0:rows, :] = features[...]
    reader = lax.broadcasted_iota(jnp.int32, (blocks, hubs), 0)
    slot = lax.broadcasted_iota(jnp.int32, (blocks, hubs), 1)
    counts = jnp.zeros((blocks, hubs), jnp.int32)
    for i in range(blocks):
        counts = jnp.where(reader == i, hub_count[0, i], counts)
    lists = jnp.where(slot < counts, hub_list[...], -1).astype(F32)
    xsend[rows:, :] = jnp.full((blocks, width), -1.0, BF16)
    xsend[rows:, 0:hubs] = lists.astype(BF16)

    pl.semaphore_wait(barrier, blocks)

    def x_copy(d):
        target = ((k + reach * r + d) % chips) * 2 + c
        return remote(xsend, xbuf.at[2 * d], xs.at[d], xr.at[2 * d], {"blk": target})

    def x_extra():
        target = ((k + reach * r + reach) % chips) * 2
        return remote(xsend, xbuf.at[half - 1], xs.at[reach], xr.at[half - 1], {"blk": target})

    def x_pass(d):
        place = 2 * d + 1 - 2 * c
        return remote(xbuf.at[2 * d], xbuf.at[place], fs.at[d], xr.at[place], partner)

    def x_wait(o):
        pltpu.make_async_copy(xbuf.at[o], xbuf.at[o], xr.at[o]).wait()

    @pl.when(r == 0)
    def _():
        pltpu.make_async_copy(xsend, xbuf.at[0], xr.at[0]).start()

    @pl.when(r == 1)
    def _():
        x_copy(0).start()

    for d in range(1, reach):
        x_copy(d).start()

    @pl.when(c == 1)
    def _():
        x_extra().start()

    def code_body(i, carry):
        o, t = i // slots, i % slots
        live = t < tile_count[0, o]
        codes[i] = jnp.where(live, tile_target[o, t] * 2 + tile_source[o, t], -1)
        return carry

    lax.fori_loop(0, half * slots, code_body, 0)

    step = 32

    def build(o, carry):
        pltpu.make_async_copy(tile_values.at[o], tiles.at[o], tile_sem.at[o]).wait()
        for first in range(0, tile, step):
            sums = [jnp.zeros((step, tile), F32) for _ in range(4)]
            for t in range(slots):
                code = codes[o * slots + t]
                value = tiles[o, t, first : first + step, :].astype(F32)
                for q in range(4):
                    sums[q] = sums[q] + value * (code == q).astype(F32)
            for q in range(4):
                i, j = q // 2, q % 2
                dense[o, i * tile + first : i * tile + first + step, j * tile : (j + 1) * tile] = sums[
                    q
                ].astype(BF16)
        return carry

    for d in range(reach):
        lax.fori_loop(2 * d, 2 * d + 2, build, 0)
        x_wait(2 * d)
        if d == 0:

            @pl.when(c == 0)
            def _():
                x_pass(0).start()

        else:
            x_pass(d).start()

    node = lax.broadcasted_iota(jnp.int32, (rows, width), 0).astype(F32)
    reader_row = lax.broadcasted_iota(jnp.int32, (blocks, width), 0)
    total[...] = jnp.zeros_like(total)

    def forward(o):
        lists = xbuf[o, rows:, :].astype(F32)
        mine = jnp.sum(jnp.where(reader_row == me, lists, 0.0), axis=0, keepdims=True)
        chosen = jnp.where(node == mine, 1.0, 0.0).astype(BF16)
        pick[o] = chosen
        block = xbuf[o, 0:rows, :]
        hub_rows = mm(chosen, block, 0, 0)
        rows_all[o * hubs : (o + 1) * hubs, :] = hub_rows[0:hubs, :].astype(BF16)
        source = (me - half * r - o + 2 * blocks) % blocks
        weight_all[o * hubs : (o + 1) * hubs, :] = hub_weight[source]
        total[...] += mm(dense[o], block)

    for o in range(0, half, 2):
        forward(o)
    for o in range(1, half, 2):
        x_wait(o)
        forward(o)
    part_send[...] = total[...] + mm(weight_all[...], rows_all[...], 0, 0)
    part = remote(part_send, part_recv, rep_s.at[0], rep_r.at[0], other_rep)
    part.start()
    own = mm(features[...], self_weight[...]) + bias[...]
    part.wait()
    aggregate[...] = (part_send[...] + part_recv[...]).astype(BF16)
    pre = own + mm(aggregate[...], neighbor_weight[...])
    gate = 1.0 / (1.0 + jnp.exp(-pre))
    output[...] = (pre * gate).astype(BF16)
    grad_act[...] = (cotangent[...].astype(F32) * gate * (1.0 + pre * (1.0 - gate))).astype(BF16)
    back_send[...] = mm(grad_act[...], neighbor_weight[...], 1, 1)
    back = remote(back_send, back_recv, rep_s.at[1], rep_r.at[1], other_rep)
    back.start()

    chunk = 2 * width // blocks
    padded = w_out.shape[1]
    sums = (mm(features[...], grad_act[...], 0, 0), mm(aggregate[...], grad_act[...], 0, 0))
    column = jnp.sum(grad_act[...].astype(F32), axis=0, keepdims=True)
    column = jnp.broadcast_to(column, (8, column.shape[1]))
    for i in range(blocks):
        which, at = (i * chunk) // width, (i * chunk) % width
        if padded > chunk:
            w_send[i, 0:padded, :] = jnp.zeros((padded, width), F32)
        w_send[i, 0:chunk, :] = sums[which][at : at + chunk, :]
        w_send[i, padded : padded + 8, :] = column
    w_recv[me] = w_send[me]

    def w_first(i):
        peer = (me + i) % blocks
        return remote(w_send.at[peer], w_recv.at[me], w1s.at[i], w1r.at[me], {"blk": peer})

    def w_second(i):
        peer = (me + i) % blocks
        return remote(w_sum, w_out.at[me], w2s.at[i], w2r.at[me], {"blk": peer})

    def run(body, low, high):
        def wrapped(i, carry):
            body(i)
            return carry

        lax.fori_loop(low, high, wrapped, 0)

    run(lambda i: w_first(i).start(), 1, blocks)
    back.wait()
    grad_aggregate = (back_send[...] + back_recv[...]).astype(BF16)
    hub_back = mm(weight_all[...], grad_aggregate).astype(BF16)

    def backward(o):
        return mm(dense[o], grad_aggregate, 0, 0) + mm(
            pick[o][:, 0:hubs], hub_back[o * hubs : (o + 1) * hubs, :]
        )

    def pair_copy(d):
        place = d + 1 - c
        return remote(pair_send.at[d], pair_recv.at[place], ps.at[d], pr.at[place], partner)

    def lone_copy():
        target = ((k - reach * r - reach + 2 * chips) % chips) * 2 + 1
        return remote(
            pair_send.at[reach - 1], src_recv.at[reach], ps.at[reach - 1], cr.at[reach], {"blk": target}
        )

    def pair_wait(d):
        pltpu.make_async_copy(pair_recv.at[d], pair_recv.at[d], pr.at[d]).wait()

    def src_copy(d):
        target = ((k - reach * r - d + 2 * chips) % chips) * 2 + c
        return remote(src_send.at[d], src_recv.at[d], cs.at[d], cr.at[d], {"blk": target})

    def src_wait(d):
        pltpu.make_async_copy(src_recv.at[d], src_recv.at[d], cr.at[d]).wait()

    for d in range(reach - 1, -1, -1):
        pair_send[d] = backward(2 * d + 1).astype(BF16)
        if d == reach - 1:

            @pl.when(c == 0)
            def _():
                lone_copy().start()

            @pl.when(c == 1)
            def _():
                pair_copy(reach - 1).start()

        else:
            pair_copy(d).start()
    for d in range(reach - 1, -1, -1):
        if d > 0:
            term = backward(2 * d)
            pair_wait(d)
            src_send[d] = (term + pair_recv[d].astype(F32)).astype(BF16)
            src_copy(d).start()
        else:
            total[...] = backward(0)

            @pl.when(c == 0)
            def _():
                pair_wait(0)
                total[...] += pair_recv[0].astype(F32)

            src_send[0] = total[...].astype(BF16)

            @pl.when(r == 0)
            def _():
                pltpu.make_async_copy(src_send.at[0], src_recv.at[0], cr.at[0]).start()

            @pl.when(r == 1)
            def _():
                src_copy(0).start()

    def w_wait_first(i):
        peer = (me + i) % blocks
        pltpu.make_async_copy(w_recv.at[peer], w_recv.at[peer], w1r.at[peer]).wait()

    run(w_wait_first, 1, blocks)
    reduced = w_recv[0]
    for i in range(1, blocks):
        reduced = reduced + w_recv[i]
    reduced = reduced * grad_scale
    w_sum[...] = reduced[0:padded, :]
    grad_bias[...] = reduced[padded : padded + 1, :]
    w_out[me] = reduced[0:padded, :]
    run(lambda i: w_second(i).start(), 1, blocks)

    total[...] = mm(grad_act[...], self_weight[...], 1, 1)
    for d in range(reach):
        src_wait(d)
        total[...] += src_recv[d].astype(F32)

    @pl.when(c == 1)
    def _():
        src_wait(reach)
        total[...] += src_recv[reach].astype(F32)

    last_send[...] = total[...]
    last = remote(last_send, last_recv, rep_s.at[2], rep_r.at[2], other_rep)
    last.start()

    def w_wait_second(i):
        peer = (me + i) % blocks
        pltpu.make_async_copy(w_out.at[peer], w_out.at[peer], w2r.at[peer]).wait()

    run(w_wait_second, 1, blocks)
    for i in range(blocks):
        which, at = (i * chunk) // width, (i * chunk) % width
        (grad_self, grad_neighbor)[which][at : at + chunk, :] = w_out[i, 0:chunk, :]
    last.wait()
    grad_input[...] = (last_send[...] + last_recv[...]).astype(BF16)

    @pl.when(r == 1)
    def _():
        x_copy(0).wait_send()
        src_copy(0).wait_send()

    for d in range(1, reach):
        x_copy(d).wait_send()
        x_pass(d).wait_send()
        src_copy(d).wait_send()

    for d in range(reach - 1):
        pair_copy(d).wait_send()

    @pl.when(c == 0)
    def _():
        x_pass(0).wait_send()
        lone_copy().wait_send()

    @pl.when(c == 1)
    def _():
        x_extra().wait_send()
        pair_copy(reach - 1).wait_send()

    run(lambda i: w_first(i).wait_send(), 1, blocks)
    run(lambda i: w_second(i).wait_send(), 1, blocks)


def on_device(
    features, tile_values, tile_target, tile_source, tile_count, hub_list, hub_count, hub_weight,
    self_weight, neighbor_weight, bias, cotangent,
):
    blocks = lax.axis_size("blk")
    rows, width = features.shape
    half, slots, tile = tile_values.shape[1:4]
    hubs = hub_list.shape[-1]
    hidden = self_weight.shape[1]
    reach = half // 2
    chunk = 2 * width // blocks
    padded = max(chunk, 8)
    grad_scale = 1.0 / math.sqrt(rows * blocks)
    vmem = pl.BlockSpec(memory_space=pltpu.VMEM)
    smem = pl.BlockSpec(memory_space=pltpu.SMEM)
    dma = pltpu.SemaphoreType.DMA
    V = pltpu.VMEM
    block = (rows, width)
    scratch = [
        V((half, slots, tile, tile), BF16),
        V((half, rows, rows), BF16),
        V((rows + blocks, width), BF16),
        V((half, rows + blocks, width), BF16),
        V((half, rows, width), BF16),
        V((half * hubs, width), BF16),
        V((half * hubs, rows), BF16),
        V(block, F32),
        pltpu.SMEM((half * slots,), jnp.int32),
        V(block, F32), V(block, F32),
        V(block, F32), V(block, F32),
        V(block, F32), V(block, F32),
        V(block, BF16),
        V((rows, hidden), BF16),
        V((reach,) + block, BF16), V((reach,) + block, BF16),
        V((reach,) + block, BF16), V((reach + 1,) + block, BF16),
        V((blocks, padded + 8, hidden), F32), V((blocks, padded + 8, hidden), F32),
        V((padded, hidden), F32), V((blocks, padded, hidden), F32),
        dma((half,)),
        dma((reach + 1,)), dma((half,)), dma((reach,)),
        dma((3,)), dma((3,)),
        dma((reach,)), dma((reach,)),
        dma((reach,)), dma((reach + 1,)),
        dma((blocks,)), dma((blocks,)), dma((blocks,)), dma((blocks,)),
    ]
    out = pl.pallas_call(
        functools.partial(kernel, blocks, grad_scale),
        out_shape=(
            jax.ShapeDtypeStruct((rows, hidden), BF16),
            jax.ShapeDtypeStruct((rows, width), BF16),
            jax.ShapeDtypeStruct((width, hidden), F32),
            jax.ShapeDtypeStruct((width, hidden), F32),
            jax.ShapeDtypeStruct((1, hidden), F32),
        ),
        in_specs=[
            vmem, pl.BlockSpec(memory_space=pl.ANY), smem, smem, smem, vmem, smem, vmem,
            vmem, vmem, vmem, vmem,
        ],
        out_specs=(vmem,) * 5,
        scratch_shapes=scratch,
        compiler_params=pltpu.CompilerParams(
            collective_id=0, has_side_effects=True, vmem_limit_bytes=56 * 1024 * 1024
        ),
    )(
        features, tile_values[0], tile_target[0], tile_source[0], tile_count, hub_list[0],
        hub_count, hub_weight, self_weight, neighbor_weight, bias.reshape(1, hidden), cotangent,
    )
    return out[0], out[1], out[2], out[3], out[4].reshape(hidden)


def solution(mesh):
    in_specs = (
        P("blk", None),
        P("blk", "rep", None, None, None),
        P("blk", "rep", None),
        P("blk", "rep", None),
        P("blk", "rep"),
        P("blk", None, None),
        P("blk", None),
        P(None, None, "blk"),
        P(None, "rep"),
        P(None, "rep"),
        P("rep"),
        P("blk", "rep"),
    )
    out_specs = (P("blk", "rep"), P("blk", None), P(None, "rep"), P(None, "rep"), P("rep"))
    return jax.shard_map(
        on_device, mesh=mesh, in_specs=in_specs, out_specs=out_specs, check_vma=False
    )
```

```python
import functools
import math

import jax
import jax.numpy as jnp
from jax import lax
from jax.experimental import pallas as pl
from jax.experimental.pallas import tpu as pltpu
from jax.sharding import PartitionSpec as P

MESH = pl.DeviceIdType.MESH
F32 = jnp.float32
BF16 = jnp.bfloat16


def mm(a, b, ca=1, cb=0):
    return lax.dot_general(a, b, (((ca,), (cb,)), ((), ())), preferred_element_type=F32)


def remote(src, dst, send, recv, device):
    return pltpu.make_async_remote_copy(
        src_ref=src, dst_ref=dst, send_sem=send, recv_sem=recv, device_id=device, device_id_type=MESH
    )


def kernel(
    blocks, grad_scale,
    features, tile_values, tile_target, tile_source, tile_count, hub_list, hub_count, hub_weight,
    self_weight, neighbor_weight, bias, cotangent,
    output, grad_input, grad_self, grad_neighbor, grad_bias,
    tiles, dense, xsend, xbuf, pick, rows_all, weight_all, total, codes,
    part_send, part_recv, back_send, back_recv, last_send, last_recv,
    aggregate, grad_act, pair_send, pair_recv, src_send, src_recv,
    w_send, w_recv, w_sum, w_out,
    tile_sem, xs, xr, fs, rep_s, rep_r, ps, pr, cs, cr, w1s, w1r, w2s, w2r,
):
    half = tile_values.shape[0]
    slots = tile_values.shape[1]
    tile = tile_values.shape[2]
    rows = features.shape[0]
    width = features.shape[1]
    hubs = hub_list.shape[1]
    chips = blocks // 2
    reach = half // 2
    me = lax.axis_index("blk")
    r = lax.axis_index("rep")
    k = me // 2
    c = me % 2
    partner = {"blk": k * 2 + 1 - c}
    other_rep = {"rep": 1 - r}

    for o in range(half):
        pltpu.make_async_copy(tile_values.at[o], tiles.at[o], tile_sem.at[o]).start()
    barrier = pltpu.get_barrier_semaphore()

    def greet(i, carry):
        pl.semaphore_signal(
            barrier, inc=1, device_id={"blk": (me + i) % blocks}, device_id_type=MESH
        )
        return carry

    lax.fori_loop(1, blocks, greet, 0)
    pl.semaphore_signal(barrier, inc=1, device_id=other_rep, device_id_type=MESH)

    xsend[0:rows, :] = features[...]
    reader = lax.broadcasted_iota(jnp.int32, (blocks, hubs), 0)
    slot = lax.broadcasted_iota(jnp.int32, (blocks, hubs), 1)
    counts = jnp.zeros((blocks, hubs), jnp.int32)
    for i in range(blocks):
        counts = jnp.where(reader == i, hub_count[0, i], counts)
    lists = jnp.where(slot < counts, hub_list[...], -1).astype(F32)
    xsend[rows:, :] = jnp.full((blocks, width), -1.0, BF16)
    xsend[rows:, 0:hubs] = lists.astype(BF16)

    pl.semaphore_wait(barrier, blocks)

    def x_copy(d):
        target = ((k + reach * r + d) % chips) * 2 + c
        return remote(xsend, xbuf.at[2 * d], xs.at[d], xr.at[2 * d], {"blk": target})

    def x_extra():
        target = ((k + reach * r + reach) % chips) * 2
        return remote(xsend, xbuf.at[half - 1], xs.at[reach], xr.at[half - 1], {"blk": target})

    def x_pass(d):
        place = 2 * d + 1 - 2 * c
        return remote(xbuf.at[2 * d], xbuf.at[place], fs.at[d], xr.at[place], partner)

    def x_wait(o):
        pltpu.make_async_copy(xbuf.at[o], xbuf.at[o], xr.at[o]).wait()

    @pl.when(r == 0)
    def _():
        pltpu.make_async_copy(xsend, xbuf.at[0], xr.at[0]).start()

    @pl.when(r == 1)
    def _():
        x_copy(0).start()

    for d in range(1, reach):
        x_copy(d).start()

    @pl.when(c == 1)
    def _():
        x_extra().start()

    def code_body(i, carry):
        o, t = i // slots, i % slots
        live = t < tile_count[0, o]
        codes[i] = jnp.where(live, tile_target[o, t] * 2 + tile_source[o, t], -1)
        return carry

    lax.fori_loop(0, half * slots, code_body, 0)

    step = 32

    def build(o, carry):
        pltpu.make_async_copy(tile_values.at[o], tiles.at[o], tile_sem.at[o]).wait()
        for first in range(0, tile, step):
            sums = [jnp.zeros((step, tile), F32) for _ in range(4)]
            for t in range(slots):
                code = codes[o * slots + t]
                value = tiles[o, t, first : first + step, :].astype(F32)
                for q in range(4):
                    sums[q] = sums[q] + value * (code == q).astype(F32)
            for q in range(4):
                i, j = q // 2, q % 2
                dense[o, i * tile + first : i * tile + first + step, j * tile : (j + 1) * tile] = sums[
                    q
                ].astype(BF16)
        return carry

    for d in range(reach):
        lax.fori_loop(2 * d, 2 * d + 2, build, 0)
        x_wait(2 * d)
        if d == 0:

            @pl.when(c == 0)
            def _():
                x_pass(0).start()

        else:
            x_pass(d).start()

    node = lax.broadcasted_iota(jnp.int32, (rows, width), 0).astype(F32)
    reader_row = lax.broadcasted_iota(jnp.int32, (blocks, width), 0)
    total[...] = jnp.zeros_like(total)

    def forward(o):
        lists = xbuf[o, rows:, :].astype(F32)
        mine = jnp.sum(jnp.where(reader_row == me, lists, 0.0), axis=0, keepdims=True)
        chosen = jnp.where(node == mine, 1.0, 0.0).astype(BF16)
        pick[o] = chosen
        block = xbuf[o, 0:rows, :]
        hub_rows = mm(chosen, block, 0, 0)
        rows_all[o * hubs : (o + 1) * hubs, :] = hub_rows[0:hubs, :].astype(BF16)
        source = (me - half * r - o + 2 * blocks) % blocks
        weight_all[o * hubs : (o + 1) * hubs, :] = hub_weight[source]
        total[...] += mm(dense[o], block)

    for o in range(0, half, 2):
        forward(o)
    for o in range(1, half, 2):
        x_wait(o)
        forward(o)
    part_send[...] = total[...] + mm(weight_all[...], rows_all[...], 0, 0)
    part = remote(part_send, part_recv, rep_s.at[0], rep_r.at[0], other_rep)
    part.start()
    own = mm(features[...], self_weight[...]) + bias[...]
    part.wait()
    aggregate[...] = (part_send[...] + part_recv[...]).astype(BF16)
    pre = own + mm(aggregate[...], neighbor_weight[...])
    gate = 1.0 / (1.0 + jnp.exp(-pre))
    output[...] = (pre * gate).astype(BF16)
    grad_act[...] = (cotangent[...].astype(F32) * gate * (1.0 + pre * (1.0 - gate))).astype(BF16)
    back_send[...] = mm(grad_act[...], neighbor_weight[...], 1, 1)
    back = remote(back_send, back_recv, rep_s.at[1], rep_r.at[1], other_rep)
    back.start()

    chunk = 2 * width // blocks
    padded = w_out.shape[1]
    sums = (mm(features[...], grad_act[...], 0, 0), mm(aggregate[...], grad_act[...], 0, 0))
    column = jnp.sum(grad_act[...].astype(F32), axis=0, keepdims=True)
    column = jnp.broadcast_to(column, (8, column.shape[1]))
    for i in range(blocks):
        which, at = (i * chunk) // width, (i * chunk) % width
        if padded > chunk:
            w_send[i, 0:padded, :] = jnp.zeros((padded, width), F32)
        w_send[i, 0:chunk, :] = sums[which][at : at + chunk, :]
        w_send[i, padded : padded + 8, :] = column
    w_recv[me] = w_send[me]

    def w_first(i):
        peer = (me + i) % blocks
        return remote(w_send.at[peer], w_recv.at[me], w1s.at[i], w1r.at[me], {"blk": peer})

    def w_second(i):
        peer = (me + i) % blocks
        return remote(w_sum, w_out.at[me], w2s.at[i], w2r.at[me], {"blk": peer})

    def run(body, low, high):
        def wrapped(i, carry):
            body(i)
            return carry

        lax.fori_loop(low, high, wrapped, 0)

    run(lambda i: w_first(i).start(), 1, blocks)
    back.wait()
    grad_aggregate = (back_send[...] + back_recv[...]).astype(BF16)
    hub_back = mm(weight_all[...], grad_aggregate).astype(BF16)

    def backward(o):
        return mm(dense[o], grad_aggregate, 0, 0) + mm(
            pick[o][:, 0:hubs], hub_back[o * hubs : (o + 1) * hubs, :]
        )

    def pair_copy(d):
        place = d + 1 - c
        return remote(pair_send.at[d], pair_recv.at[place], ps.at[d], pr.at[place], partner)

    def lone_copy():
        target = ((k - reach * r - reach + 2 * chips) % chips) * 2 + 1
        return remote(
            pair_send.at[reach - 1], src_recv.at[reach], ps.at[reach - 1], cr.at[reach], {"blk": target}
        )

    def pair_wait(d):
        pltpu.make_async_copy(pair_recv.at[d], pair_recv.at[d], pr.at[d]).wait()

    def src_copy(d):
        target = ((k - reach * r - d + 2 * chips) % chips) * 2 + c
        return remote(src_send.at[d], src_recv.at[d], cs.at[d], cr.at[d], {"blk": target})

    def src_wait(d):
        pltpu.make_async_copy(src_recv.at[d], src_recv.at[d], cr.at[d]).wait()

    for d in range(reach - 1, -1, -1):
        pair_send[d] = backward(2 * d + 1).astype(BF16)
        if d == reach - 1:

            @pl.when(c == 0)
            def _():
                lone_copy().start()

            @pl.when(c == 1)
            def _():
                pair_copy(reach - 1).start()

        else:
            pair_copy(d).start()
    for d in range(reach - 1, -1, -1):
        if d > 0:
            term = backward(2 * d)
            pair_wait(d)
            src_send[d] = (term + pair_recv[d].astype(F32)).astype(BF16)
            src_copy(d).start()
        else:
            total[...] = backward(0)

            @pl.when(c == 0)
            def _():
                pair_wait(0)
                total[...] += pair_recv[0].astype(F32)

            src_send[0] = total[...].astype(BF16)

            @pl.when(r == 0)
            def _():
                pltpu.make_async_copy(src_send.at[0], src_recv.at[0], cr.at[0]).start()

            @pl.when(r == 1)
            def _():
                src_copy(0).start()

    def w_wait_first(i):
        peer = (me + i) % blocks
        pltpu.make_async_copy(w_recv.at[peer], w_recv.at[peer], w1r.at[peer]).wait()

    run(w_wait_first, 1, blocks)
    reduced = w_recv[0]
    for i in range(1, blocks):
        reduced = reduced + w_recv[i]
    reduced = reduced * grad_scale
    w_sum[...] = reduced[0:padded, :]
    grad_bias[...] = reduced[padded : padded + 1, :]
    w_out[me] = reduced[0:padded, :]
    run(lambda i: w_second(i).start(), 1, blocks)

    total[...] = mm(grad_act[...], self_weight[...], 1, 1)
    for d in range(reach):
        src_wait(d)
        total[...] += src_recv[d].astype(F32)

    @pl.when(c == 1)
    def _():
        src_wait(reach)
        total[...] += src_recv[reach].astype(F32)

    last_send[...] = total[...]
    last = remote(last_send, last_recv, rep_s.at[2], rep_r.at[2], other_rep)
    last.start()

    def w_wait_second(i):
        peer = (me + i) % blocks
        pltpu.make_async_copy(w_out.at[peer], w_out.at[peer], w2r.at[peer]).wait()

    run(w_wait_second, 1, blocks)
    for i in range(blocks):
        which, at = (i * chunk) // width, (i * chunk) % width
        (grad_self, grad_neighbor)[which][at : at + chunk, :] = w_out[i, 0:chunk, :]
    last.wait()
    grad_input[...] = (last_send[...] + last_recv[...]).astype(BF16)

    @pl.when(r == 1)
    def _():
        x_copy(0).wait_send()
        src_copy(0).wait_send()

    for d in range(1, reach):
        x_copy(d).wait_send()
        x_pass(d).wait_send()
        src_copy(d).wait_send()

    for d in range(reach - 1):
        pair_copy(d).wait_send()

    @pl.when(c == 0)
    def _():
        x_pass(0).wait_send()
        lone_copy().wait_send()

    @pl.when(c == 1)
    def _():
        x_extra().wait_send()
        pair_copy(reach - 1).wait_send()

    run(lambda i: w_first(i).wait_send(), 1, blocks)
    run(lambda i: w_second(i).wait_send(), 1, blocks)


def finish(*refs):
    for source, target in zip(refs[:5], refs[5:]):
        target[...] = source[...]


def on_device(
    features, tile_values, tile_target, tile_source, tile_count, hub_list, hub_count, hub_weight,
    self_weight, neighbor_weight, bias, cotangent,
):
    blocks = lax.axis_size("blk")
    rows, width = features.shape
    half, slots, tile = tile_values.shape[1:4]
    hubs = hub_list.shape[-1]
    hidden = self_weight.shape[1]
    reach = half // 2
    chunk = 2 * width // blocks
    padded = max(chunk, 8)
    grad_scale = 1.0 / math.sqrt(rows * blocks)
    vmem = pl.BlockSpec(memory_space=pltpu.VMEM)
    smem = pl.BlockSpec(memory_space=pltpu.SMEM)
    dma = pltpu.SemaphoreType.DMA
    V = pltpu.VMEM
    block = (rows, width)
    scratch = [
        V((half, slots, tile, tile), BF16),
        V((half, rows, rows), BF16),
        V((rows + blocks, width), BF16),
        V((half, rows + blocks, width), BF16),
        V((half, rows, width), BF16),
        V((half * hubs, width), BF16),
        V((half * hubs, rows), BF16),
        V(block, F32),
        pltpu.SMEM((half * slots,), jnp.int32),
        V(block, F32), V(block, F32),
        V(block, F32), V(block, F32),
        V(block, F32), V(block, F32),
        V(block, BF16),
        V((rows, hidden), BF16),
        V((reach,) + block, BF16), V((reach,) + block, BF16),
        V((reach,) + block, BF16), V((reach + 1,) + block, BF16),
        V((blocks, padded + 8, hidden), F32), V((blocks, padded + 8, hidden), F32),
        V((padded, hidden), F32), V((blocks, padded, hidden), F32),
        dma((half,)),
        dma((reach + 1,)), dma((half,)), dma((reach,)),
        dma((3,)), dma((3,)),
        dma((reach,)), dma((reach,)),
        dma((reach,)), dma((reach + 1,)),
        dma((blocks,)), dma((blocks,)), dma((blocks,)), dma((blocks,)),
    ]
    out = pl.pallas_call(
        functools.partial(kernel, blocks, grad_scale),
        out_shape=(
            jax.ShapeDtypeStruct((rows, hidden), BF16),
            jax.ShapeDtypeStruct((rows, width), BF16),
            jax.ShapeDtypeStruct((width, hidden), F32),
            jax.ShapeDtypeStruct((width, hidden), F32),
            jax.ShapeDtypeStruct((1, hidden), F32),
        ),
        in_specs=[
            vmem, pl.BlockSpec(memory_space=pl.ANY), smem, smem, smem, vmem, smem, vmem,
            vmem, vmem, vmem, vmem,
        ],
        out_specs=(vmem,) * 5,
        scratch_shapes=scratch,
        compiler_params=pltpu.CompilerParams(
            collective_id=0, has_side_effects=True, vmem_limit_bytes=56 * 1024 * 1024
        ),
    )(
        features, tile_values[0], tile_target[0], tile_source[0], tile_count, hub_list[0],
        hub_count, hub_weight, self_weight, neighbor_weight, bias.reshape(1, hidden), cotangent,
    )
    out = pl.pallas_call(
        finish,
        out_shape=tuple(jax.ShapeDtypeStruct(x.shape, x.dtype) for x in out),
        in_specs=[vmem] * 5,
        out_specs=(vmem,) * 5,
    )(*out)
    return out[0], out[1], out[2], out[3], out[4].reshape(hidden)


def solution(mesh):
    in_specs = (
        P("blk", None),
        P("blk", "rep", None, None, None),
        P("blk", "rep", None),
        P("blk", "rep", None),
        P("blk", "rep"),
        P("blk", None, None),
        P("blk", None),
        P(None, None, "blk"),
        P(None, "rep"),
        P(None, "rep"),
        P("rep"),
        P("blk", "rep"),
    )
    out_specs = (P("blk", "rep"), P("blk", None), P(None, "rep"), P(None, "rep"), P("rep"))
    return jax.shard_map(
        on_device, mesh=mesh, in_specs=in_specs, out_specs=out_specs, check_vma=False
    )
```

```python
import functools
import math

import jax
import jax.numpy as jnp
from jax import lax
from jax.experimental import pallas as pl
from jax.experimental.pallas import tpu as pltpu
from jax.sharding import PartitionSpec as P

MESH = pl.DeviceIdType.MESH
F32 = jnp.float32
BF16 = jnp.bfloat16


def mm(a, b, ca=1, cb=0):
    return lax.dot_general(a, b, (((ca,), (cb,)), ((), ())), preferred_element_type=F32)


def remote(src, dst, send, recv, device):
    return pltpu.make_async_remote_copy(
        src_ref=src, dst_ref=dst, send_sem=send, recv_sem=recv, device_id=device, device_id_type=MESH
    )


def kernel(
    blocks, grad_scale,
    features, tile_values, tile_target, tile_source, tile_count, hub_list, hub_count, hub_weight,
    self_weight, neighbor_weight, bias, cotangent,
    output, grad_input, grad_self, grad_neighbor, grad_bias,
    tiles, dense, dense_t, xsend, xbuf, pick, rows_all, weight_all, weight_t, total, codes,
    part_send, part_recv, back_send, back_recv, last_send, last_recv,
    aggregate, grad_act, pair_send, pair_recv, src_send, src_recv,
    w_send, w_recv, w_sum, w_out,
    tile_sem, xs, xr, fs, rep_s, rep_r, ps, pr, cs, cr, w1s, w1r, w2s, w2r,
):
    half = tile_values.shape[0]
    slots = tile_values.shape[1]
    tile = tile_values.shape[2]
    rows = features.shape[0]
    width = features.shape[1]
    hubs = hub_list.shape[1]
    chips = blocks // 2
    reach = half // 2
    me = lax.axis_index("blk")
    r = lax.axis_index("rep")
    k = me // 2
    c = me % 2
    partner = {"blk": k * 2 + 1 - c}
    other_rep = {"rep": 1 - r}

    for o in range(half):
        pltpu.make_async_copy(tile_values.at[o], tiles.at[o], tile_sem.at[o]).start()
    barrier = pltpu.get_barrier_semaphore()

    def greet(i, carry):
        pl.semaphore_signal(
            barrier, inc=1, device_id={"blk": (me + i) % blocks}, device_id_type=MESH
        )
        return carry

    lax.fori_loop(1, blocks, greet, 0)
    pl.semaphore_signal(barrier, inc=1, device_id=other_rep, device_id_type=MESH)

    xsend[0:rows, :] = features[...]
    reader = lax.broadcasted_iota(jnp.int32, (blocks, hubs), 0)
    slot = lax.broadcasted_iota(jnp.int32, (blocks, hubs), 1)
    counts = jnp.zeros((blocks, hubs), jnp.int32)
    for i in range(blocks):
        counts = jnp.where(reader == i, hub_count[0, i], counts)
    lists = jnp.where(slot < counts, hub_list[...], -1).astype(F32)
    xsend[rows:, :] = jnp.full((blocks, width), -1.0, BF16)
    xsend[rows:, 0:hubs] = lists.astype(BF16)

    pl.semaphore_wait(barrier, blocks)

    def x_copy(d):
        target = ((k + reach * r + d) % chips) * 2 + c
        return remote(xsend, xbuf.at[2 * d], xs.at[d], xr.at[2 * d], {"blk": target})

    def x_extra():
        target = ((k + reach * r + reach) % chips) * 2
        return remote(xsend, xbuf.at[half - 1], xs.at[reach], xr.at[half - 1], {"blk": target})

    def x_pass(d):
        place = 2 * d + 1 - 2 * c
        return remote(xbuf.at[2 * d], xbuf.at[place], fs.at[d], xr.at[place], partner)

    def x_wait(o):
        pltpu.make_async_copy(xbuf.at[o], xbuf.at[o], xr.at[o]).wait()

    @pl.when(r == 0)
    def _():
        pltpu.make_async_copy(xsend, xbuf.at[0], xr.at[0]).start()

    @pl.when(r == 1)
    def _():
        x_copy(0).start()

    for d in range(1, reach):
        x_copy(d).start()

    @pl.when(c == 1)
    def _():
        x_extra().start()

    def code_body(i, carry):
        o, t = i // slots, i % slots
        live = t < tile_count[0, o]
        codes[i] = jnp.where(live, tile_target[o, t] * 2 + tile_source[o, t], -1)
        return carry

    lax.fori_loop(0, half * slots, code_body, 0)

    step = 32

    def build(o, carry):
        pltpu.make_async_copy(tile_values.at[o], tiles.at[o], tile_sem.at[o]).wait()
        for first in range(0, tile, step):
            sums = [jnp.zeros((step, tile), F32) for _ in range(4)]
            for t in range(slots):
                code = codes[o * slots + t]
                value = tiles[o, t, first : first + step, :].astype(F32)
                for q in range(4):
                    sums[q] = sums[q] + value * (code == q).astype(F32)
            for q in range(4):
                i, j = q // 2, q % 2
                dense[o, i * tile + first : i * tile + first + step, j * tile : (j + 1) * tile] = sums[
                    q
                ].astype(BF16)
        dense_t[o] = dense[o].T
        return carry

    for o in range(half):
        source = (me - half * r - o + 2 * blocks) % blocks
        weight_all[o * hubs : (o + 1) * hubs, :] = hub_weight[source]
    weight_t[...] = weight_all[...].T

    for d in range(reach):
        lax.fori_loop(2 * d, 2 * d + 2, build, 0)
        x_wait(2 * d)
        if d == 0:

            @pl.when(c == 0)
            def _():
                x_pass(0).start()

        else:
            x_pass(d).start()

    node = lax.broadcasted_iota(jnp.int32, (rows, width), 0).astype(F32)
    node_lane = lax.broadcasted_iota(jnp.int32, (hubs, rows), 1).astype(F32)
    reader_row = lax.broadcasted_iota(jnp.int32, (blocks, width), 0)
    total[...] = jnp.zeros_like(total)

    def hub_row(o):
        lists = xbuf[o, rows:, :].astype(F32)
        return jnp.sum(jnp.where(reader_row == me, lists, 0.0), axis=0, keepdims=True)

    def forward(o):
        column = jnp.broadcast_to(hub_row(o), (8, width)).T[0:hubs, 0:1]
        chosen = jnp.where(node_lane == column, 1.0, 0.0).astype(BF16)
        block = xbuf[o, 0:rows, :]
        rows_all[o * hubs : (o + 1) * hubs, :] = mm(chosen, block).astype(BF16)
        total[...] += mm(dense[o], block)

    for o in range(0, half, 2):
        forward(o)
    for o in range(1, half, 2):
        x_wait(o)
        forward(o)
    total[...] += mm(weight_t[...], rows_all[...])
    part_send[...] = total[...].astype(BF16)
    part = remote(part_send, part_recv, rep_s.at[0], rep_r.at[0], other_rep)
    part.start()
    own = mm(features[...], self_weight[...]) + bias[...]
    for o in range(half):
        pick[o] = jnp.where(node == hub_row(o), 1.0, 0.0).astype(BF16)
    part.wait()
    aggregate[...] = (total[...] + part_recv[...].astype(F32)).astype(BF16)
    pre = own + mm(aggregate[...], neighbor_weight[...])
    gate = 1.0 / (1.0 + jnp.exp(-pre))
    output[...] = (pre * gate).astype(BF16)
    grad_act[...] = (cotangent[...].astype(F32) * gate * (1.0 + pre * (1.0 - gate))).astype(BF16)
    total[...] = mm(grad_act[...], neighbor_weight[...], 1, 1)
    back_send[...] = total[...].astype(BF16)
    back = remote(back_send, back_recv, rep_s.at[1], rep_r.at[1], other_rep)
    back.start()

    chunk = 2 * width // blocks
    padded = w_out.shape[1]
    sums = (mm(features[...], grad_act[...], 0, 0), mm(aggregate[...], grad_act[...], 0, 0))
    column = jnp.sum(grad_act[...].astype(F32), axis=0, keepdims=True)
    column = jnp.broadcast_to(column, (8, column.shape[1]))
    for i in range(blocks):
        which, at = (i * chunk) // width, (i * chunk) % width
        if padded > chunk:
            w_send[i, 0:padded, :] = jnp.zeros((padded, width), F32)
        w_send[i, 0:chunk, :] = sums[which][at : at + chunk, :]
        w_send[i, padded : padded + 8, :] = column
    w_recv[me] = w_send[me]

    def w_first(i):
        peer = (me + i) % blocks
        return remote(w_send.at[peer], w_recv.at[me], w1s.at[i], w1r.at[me], {"blk": peer})

    def w_second(i):
        peer = (me + i) % blocks
        return remote(w_sum, w_out.at[me], w2s.at[i], w2r.at[me], {"blk": peer})

    def run(body, low, high):
        def wrapped(i, carry):
            body(i)
            return carry

        lax.fori_loop(low, high, wrapped, 0)

    back.wait()
    grad_aggregate = (total[...] + back_recv[...].astype(F32)).astype(BF16)
    hub_back = mm(weight_all[...], grad_aggregate).astype(BF16)

    def backward(o):
        return mm(dense_t[o], grad_aggregate) + mm(
            pick[o][:, 0:hubs], hub_back[o * hubs : (o + 1) * hubs, :]
        )

    def pair_copy(d):
        place = d + 1 - c
        return remote(pair_send.at[d], pair_recv.at[place], ps.at[d], pr.at[place], partner)

    def lone_copy():
        target = ((k - reach * r - reach + 2 * chips) % chips) * 2 + 1
        return remote(
            pair_send.at[reach - 1], src_recv.at[reach], ps.at[reach - 1], cr.at[reach], {"blk": target}
        )

    def pair_wait(d):
        pltpu.make_async_copy(pair_recv.at[d], pair_recv.at[d], pr.at[d]).wait()

    def src_copy(d):
        target = ((k - reach * r - d + 2 * chips) % chips) * 2 + c
        return remote(src_send.at[d], src_recv.at[d], cs.at[d], cr.at[d], {"blk": target})

    def src_wait(d):
        pltpu.make_async_copy(src_recv.at[d], src_recv.at[d], cr.at[d]).wait()

    for d in range(reach - 1, -1, -1):
        pair_send[d] = backward(2 * d + 1).astype(BF16)
        if d == reach - 1:

            @pl.when(c == 0)
            def _():
                lone_copy().start()

            @pl.when(c == 1)
            def _():
                pair_copy(reach - 1).start()

        else:
            pair_copy(d).start()
    run(lambda i: w_first(i).start(), 1, blocks)
    for d in range(reach - 1, -1, -1):
        if d > 0:
            term = backward(2 * d)
            pair_wait(d)
            src_send[d] = (term + pair_recv[d].astype(F32)).astype(BF16)
            src_copy(d).start()
        else:
            total[...] = backward(0)

            @pl.when(c == 0)
            def _():
                pair_wait(0)
                total[...] += pair_recv[0].astype(F32)

            src_send[0] = total[...].astype(BF16)

            @pl.when(r == 0)
            def _():
                pltpu.make_async_copy(src_send.at[0], src_recv.at[0], cr.at[0]).start()

            @pl.when(r == 1)
            def _():
                src_copy(0).start()

    def w_wait_first(i):
        peer = (me + i) % blocks
        pltpu.make_async_copy(w_recv.at[peer], w_recv.at[peer], w1r.at[peer]).wait()

    run(w_wait_first, 1, blocks)
    reduced = w_recv[0]
    for i in range(1, blocks):
        reduced = reduced + w_recv[i]
    reduced = reduced * grad_scale
    w_sum[...] = reduced[0:padded, :]
    grad_bias[...] = reduced[padded : padded + 1, :]
    w_out[me] = reduced[0:padded, :]
    run(lambda i: w_second(i).start(), 1, blocks)

    total[...] = mm(grad_act[...], self_weight[...], 1, 1)
    for d in range(reach):
        src_wait(d)
        total[...] += src_recv[d].astype(F32)

    @pl.when(c == 1)
    def _():
        src_wait(reach)
        total[...] += src_recv[reach].astype(F32)

    last_send[...] = total[...].astype(BF16)
    last = remote(last_send, last_recv, rep_s.at[2], rep_r.at[2], other_rep)
    last.start()

    def w_wait_second(i):
        peer = (me + i) % blocks
        pltpu.make_async_copy(w_out.at[peer], w_out.at[peer], w2r.at[peer]).wait()

    run(w_wait_second, 1, blocks)
    for i in range(blocks):
        which, at = (i * chunk) // width, (i * chunk) % width
        (grad_self, grad_neighbor)[which][at : at + chunk, :] = w_out[i, 0:chunk, :]
    last.wait()
    grad_input[...] = (last_send[...].astype(F32) + last_recv[...].astype(F32)).astype(BF16)

    @pl.when(r == 1)
    def _():
        x_copy(0).wait_send()
        src_copy(0).wait_send()

    for d in range(1, reach):
        x_copy(d).wait_send()
        x_pass(d).wait_send()
        src_copy(d).wait_send()

    for d in range(reach - 1):
        pair_copy(d).wait_send()

    @pl.when(c == 0)
    def _():
        x_pass(0).wait_send()
        lone_copy().wait_send()

    @pl.when(c == 1)
    def _():
        x_extra().wait_send()
        pair_copy(reach - 1).wait_send()

    run(lambda i: w_first(i).wait_send(), 1, blocks)
    run(lambda i: w_second(i).wait_send(), 1, blocks)


def finish(*refs):
    for source, target in zip(refs[:5], refs[5:]):
        target[...] = source[...]


def on_device(
    features, tile_values, tile_target, tile_source, tile_count, hub_list, hub_count, hub_weight,
    self_weight, neighbor_weight, bias, cotangent,
):
    blocks = lax.axis_size("blk")
    rows, width = features.shape
    half, slots, tile = tile_values.shape[1:4]
    hubs = hub_list.shape[-1]
    hidden = self_weight.shape[1]
    reach = half // 2
    chunk = 2 * width // blocks
    padded = max(chunk, 8)
    grad_scale = 1.0 / math.sqrt(rows * blocks)
    vmem = pl.BlockSpec(memory_space=pltpu.VMEM)
    smem = pl.BlockSpec(memory_space=pltpu.SMEM)
    dma = pltpu.SemaphoreType.DMA
    V = pltpu.VMEM
    block = (rows, width)
    scratch = [
        V((half, slots, tile, tile), BF16),
        V((half, rows, rows), BF16),
        V((half, rows, rows), BF16),
        V((rows + blocks, width), BF16),
        V((half, rows + blocks, width), BF16),
        V((half, rows, width), BF16),
        V((half * hubs, width), BF16),
        V((half * hubs, rows), BF16),
        V((rows, half * hubs), BF16),
        V(block, F32),
        pltpu.SMEM((half * slots,), jnp.int32),
        V(block, BF16), V(block, BF16),
        V(block, BF16), V(block, BF16),
        V(block, BF16), V(block, BF16),
        V(block, BF16),
        V((rows, hidden), BF16),
        V((reach,) + block, BF16), V((reach,) + block, BF16),
        V((reach,) + block, BF16), V((reach + 1,) + block, BF16),
        V((blocks, padded + 8, hidden), F32), V((blocks, padded + 8, hidden), F32),
        V((padded, hidden), F32), V((blocks, padded, hidden), F32),
        dma((half,)),
        dma((reach + 1,)), dma((half,)), dma((reach,)),
        dma((3,)), dma((3,)),
        dma((reach,)), dma((reach,)),
        dma((reach,)), dma((reach + 1,)),
        dma((blocks,)), dma((blocks,)), dma((blocks,)), dma((blocks,)),
    ]
    out = pl.pallas_call(
        functools.partial(kernel, blocks, grad_scale),
        out_shape=(
            jax.ShapeDtypeStruct((rows, hidden), BF16),
            jax.ShapeDtypeStruct((rows, width), BF16),
            jax.ShapeDtypeStruct((width, hidden), F32),
            jax.ShapeDtypeStruct((width, hidden), F32),
            jax.ShapeDtypeStruct((1, hidden), F32),
        ),
        in_specs=[
            vmem, pl.BlockSpec(memory_space=pl.ANY), smem, smem, smem, vmem, smem, vmem,
            vmem, vmem, vmem, vmem,
        ],
        out_specs=(vmem,) * 5,
        scratch_shapes=scratch,
        compiler_params=pltpu.CompilerParams(
            collective_id=0, has_side_effects=True, vmem_limit_bytes=56 * 1024 * 1024
        ),
    )(
        features, tile_values[0], tile_target[0], tile_source[0], tile_count, hub_list[0],
        hub_count, hub_weight, self_weight, neighbor_weight, bias.reshape(1, hidden), cotangent,
    )
    out = pl.pallas_call(
        finish,
        out_shape=tuple(jax.ShapeDtypeStruct(x.shape, x.dtype) for x in out),
        in_specs=[vmem] * 5,
        out_specs=(vmem,) * 5,
    )(*out)
    return out[0], out[1], out[2], out[3], out[4].reshape(hidden)


def solution(mesh):
    in_specs = (
        P("blk", None),
        P("blk", "rep", None, None, None),
        P("blk", "rep", None),
        P("blk", "rep", None),
        P("blk", "rep"),
        P("blk", None, None),
        P("blk", None),
        P(None, None, "blk"),
        P(None, "rep"),
        P(None, "rep"),
        P("rep"),
        P("blk", "rep"),
    )
    out_specs = (P("blk", "rep"), P("blk", None), P(None, "rep"), P(None, "rep"), P("rep"))
    return jax.shard_map(
        on_device, mesh=mesh, in_specs=in_specs, out_specs=out_specs, check_vma=False
    )
```

```python
import functools
import math

import jax
import jax.numpy as jnp
from jax import lax
from jax.experimental import pallas as pl
from jax.experimental.pallas import tpu as pltpu
from jax.sharding import PartitionSpec as P

MESH = pl.DeviceIdType.MESH
F32 = jnp.float32
BF16 = jnp.bfloat16


def mm(a, b, ca=1, cb=0):
    return lax.dot_general(a, b, (((ca,), (cb,)), ((), ())), preferred_element_type=F32)


def remote(src, dst, send, recv, device):
    return pltpu.make_async_remote_copy(
        src_ref=src, dst_ref=dst, send_sem=send, recv_sem=recv, device_id=device, device_id_type=MESH
    )


def kernel(
    blocks, grad_scale,
    features, tile_values, tile_target, tile_source, tile_count, hub_list, hub_count, hub_weight,
    self_weight, neighbor_weight, bias, cotangent,
    output, grad_input, grad_self, grad_neighbor, grad_bias,
    tiles, dense, dense_t, xsend, xbuf, pick, rows_all, weight_all, weight_t, total, codes,
    part_send, part_recv, back_send, back_recv, last_send, last_recv,
    aggregate, grad_act, pair_send, pair_recv, src_send, src_recv,
    w_send, w_recv, w_sum, w_out,
    tile_sem, xs, xr, fs, rl, rep_s, rep_r, ps, pr, cs, cr, w1s, w1r, w2s, w2r,
):
    half = tile_values.shape[0]
    slots = tile_values.shape[1]
    tile = tile_values.shape[2]
    rows = features.shape[0]
    width = features.shape[1]
    hubs = hub_list.shape[1]
    chips = blocks // 2
    reach = half // 2
    me = lax.axis_index("blk")
    r = lax.axis_index("rep")
    k = me // 2
    c = me % 2
    partner = {"blk": k * 2 + 1 - c}
    other_rep = {"rep": 1 - r}

    for o in range(half):
        pltpu.make_async_copy(tile_values.at[o], tiles.at[o], tile_sem.at[o]).start()
    barrier = pltpu.get_barrier_semaphore()

    def greet(i, carry):
        pl.semaphore_signal(
            barrier, inc=1, device_id={"blk": (me + i) % blocks}, device_id_type=MESH
        )
        return carry

    lax.fori_loop(1, blocks, greet, 0)
    pl.semaphore_signal(barrier, inc=1, device_id=other_rep, device_id_type=MESH)

    xsend[0:rows, :] = features[...]
    reader = lax.broadcasted_iota(jnp.int32, (blocks, hubs), 0)
    slot = lax.broadcasted_iota(jnp.int32, (blocks, hubs), 1)
    counts = jnp.zeros((blocks, hubs), jnp.int32)
    for i in range(blocks):
        counts = jnp.where(reader == i, hub_count[0, i], counts)
    lists = jnp.where(slot < counts, hub_list[...], -1).astype(F32)
    xsend[rows:, :] = jnp.full((blocks, width), -1.0, BF16)
    xsend[rows:, 0:hubs] = lists.astype(BF16)

    pl.semaphore_wait(barrier, blocks)

    def x_copy(d):
        target = ((k + reach * r + d) % chips) * 2 + c
        return remote(xsend, xbuf.at[2 * d], xs.at[d], xr.at[2 * d], {"blk": target})

    def x_extra():
        target = ((k + reach * r + reach) % chips) * 2
        return remote(xsend, xbuf.at[half - 1], xs.at[reach], xr.at[half - 1], {"blk": target})

    def x_pass(d):
        place = 2 * d + 1 - 2 * c
        return remote(xbuf.at[2 * d], xbuf.at[place], fs.at[d], xr.at[place], partner)

    def x_direct(d):
        return (k + reach * r + d) % 2 == 0

    def x_relay(d):
        return remote(
            xbuf.at[2 * d], xbuf.at[2 * d + 2], rl.at[d], xr.at[2 * d + 2], {"blk": (me + 2) % blocks}
        )

    def x_wait(o):
        pltpu.make_async_copy(xbuf.at[o], xbuf.at[o], xr.at[o]).wait()

    @pl.when(r == 0)
    def _():
        pltpu.make_async_copy(xsend, xbuf.at[0], xr.at[0]).start()

    @pl.when(r == 1)
    def _():
        x_copy(0).start()

    for d in range(1, reach):

        @pl.when(x_direct(d))
        def _():
            x_copy(d).start()

    @pl.when(c == 1)
    def _():
        x_extra().start()

    def code_body(i, carry):
        o, t = i // slots, i % slots
        live = t < tile_count[0, o]
        codes[i] = jnp.where(live, tile_target[o, t] * 2 + tile_source[o, t], -1)
        return carry

    lax.fori_loop(0, half * slots, code_body, 0)

    step = 32

    def build(o, carry):
        pltpu.make_async_copy(tile_values.at[o], tiles.at[o], tile_sem.at[o]).wait()
        for first in range(0, tile, step):
            sums = [jnp.zeros((step, tile), F32) for _ in range(4)]
            for t in range(slots):
                code = codes[o * slots + t]
                value = tiles[o, t, first : first + step, :].astype(F32)
                for q in range(4):
                    sums[q] = sums[q] + value * (code == q).astype(F32)
            for q in range(4):
                i, j = q // 2, q % 2
                dense[o, i * tile + first : i * tile + first + step, j * tile : (j + 1) * tile] = sums[
                    q
                ].astype(BF16)
        dense_t[o] = dense[o].T
        return carry

    for o in range(half):
        source = (me - half * r - o + 2 * blocks) % blocks
        weight_all[o * hubs : (o + 1) * hubs, :] = hub_weight[source]
    weight_t[...] = weight_all[...].T

    for d in range(reach):
        lax.fori_loop(2 * d, 2 * d + 2, build, 0)
        x_wait(2 * d)
        if d < reach - 1:

            @pl.when(k % 2 == 0)
            def _():
                x_relay(d).start()

        if d == 0:

            @pl.when(c == 0)
            def _():
                x_pass(0).start()

        else:
            x_pass(d).start()

    node = lax.broadcasted_iota(jnp.int32, (rows, width), 0).astype(F32)
    node_lane = lax.broadcasted_iota(jnp.int32, (hubs, rows), 1).astype(F32)
    reader_row = lax.broadcasted_iota(jnp.int32, (blocks, width), 0)
    total[...] = jnp.zeros_like(total)

    def hub_row(o):
        lists = xbuf[o, rows:, :].astype(F32)
        return jnp.sum(jnp.where(reader_row == me, lists, 0.0), axis=0, keepdims=True)

    def forward(o):
        column = jnp.broadcast_to(hub_row(o), (8, width)).T[0:hubs, 0:1]
        chosen = jnp.where(node_lane == column, 1.0, 0.0).astype(BF16)
        block = xbuf[o, 0:rows, :]
        rows_all[o * hubs : (o + 1) * hubs, :] = mm(chosen, block).astype(BF16)
        total[...] += mm(dense[o], block)

    for o in range(0, half, 2):
        forward(o)
    for o in range(1, half, 2):
        x_wait(o)
        forward(o)
    total[...] += mm(weight_t[...], rows_all[...])
    part_send[...] = total[...].astype(BF16)
    part = remote(part_send, part_recv, rep_s.at[0], rep_r.at[0], other_rep)
    part.start()
    own = mm(features[...], self_weight[...]) + bias[...]
    for o in range(half):
        pick[o] = jnp.where(node == hub_row(o), 1.0, 0.0).astype(BF16)
    part.wait()
    aggregate[...] = (total[...] + part_recv[...].astype(F32)).astype(BF16)
    pre = own + mm(aggregate[...], neighbor_weight[...])
    gate = 1.0 / (1.0 + jnp.exp(-pre))
    output[...] = (pre * gate).astype(BF16)
    grad_act[...] = (cotangent[...].astype(F32) * gate * (1.0 + pre * (1.0 - gate))).astype(BF16)
    total[...] = mm(grad_act[...], neighbor_weight[...], 1, 1)
    back_send[...] = total[...].astype(BF16)
    back = remote(back_send, back_recv, rep_s.at[1], rep_r.at[1], other_rep)
    back.start()

    chunk = 2 * width // blocks
    padded = w_out.shape[1]
    sums = (mm(features[...], grad_act[...], 0, 0), mm(aggregate[...], grad_act[...], 0, 0))
    column = jnp.sum(grad_act[...].astype(F32), axis=0, keepdims=True)
    column = jnp.broadcast_to(column, (8, column.shape[1]))
    for i in range(blocks):
        which, at = (i * chunk) // width, (i * chunk) % width
        if padded > chunk:
            w_send[i, 0:padded, :] = jnp.zeros((padded, width), F32)
        w_send[i, 0:chunk, :] = sums[which][at : at + chunk, :]
        w_send[i, padded : padded + 8, :] = column
    w_recv[me] = w_send[me]

    def w_first(i):
        peer = (me + i) % blocks
        return remote(w_send.at[peer], w_recv.at[me], w1s.at[i], w1r.at[me], {"blk": peer})

    def w_second(i):
        peer = (me + i) % blocks
        return remote(w_sum, w_out.at[me], w2s.at[i], w2r.at[me], {"blk": peer})

    def run(body, low, high):
        def wrapped(i, carry):
            body(i)
            return carry

        lax.fori_loop(low, high, wrapped, 0)

    back.wait()
    grad_aggregate = (total[...] + back_recv[...].astype(F32)).astype(BF16)
    hub_back = mm(weight_all[...], grad_aggregate).astype(BF16)

    def backward(o):
        return mm(dense_t[o], grad_aggregate) + mm(
            pick[o][:, 0:hubs], hub_back[o * hubs : (o + 1) * hubs, :]
        )

    def pair_copy(d):
        place = d + 1 - c
        return remote(pair_send.at[d], pair_recv.at[place], ps.at[d], pr.at[place], partner)

    def lone_copy():
        target = ((k - reach * r - reach + 2 * chips) % chips) * 2 + 1
        return remote(
            pair_send.at[reach - 1], src_recv.at[reach], ps.at[reach - 1], cr.at[reach], {"blk": target}
        )

    def pair_wait(d):
        pltpu.make_async_copy(pair_recv.at[d], pair_recv.at[d], pr.at[d]).wait()

    def src_copy(d):
        target = ((k - reach * r - d + 2 * chips) % chips) * 2 + c
        return remote(src_send.at[d], src_recv.at[d], cs.at[d], cr.at[d], {"blk": target})

    def src_wait(d):
        pltpu.make_async_copy(src_recv.at[d], src_recv.at[d], cr.at[d]).wait()

    for d in range(reach - 1, -1, -1):
        pair_send[d] = backward(2 * d + 1).astype(BF16)
        if d == reach - 1:

            @pl.when(c == 0)
            def _():
                lone_copy().start()

            @pl.when(c == 1)
            def _():
                pair_copy(reach - 1).start()

        else:
            pair_copy(d).start()
    for d in range(reach - 1, -1, -1):
        if d > 0:
            term = backward(2 * d)
            pair_wait(d)
            src_send[d] = (term + pair_recv[d].astype(F32)).astype(BF16)
            src_copy(d).start()
        else:
            total[...] = backward(0)

            @pl.when(c == 0)
            def _():
                pair_wait(0)
                total[...] += pair_recv[0].astype(F32)

            src_send[0] = total[...].astype(BF16)

            @pl.when(r == 0)
            def _():
                pltpu.make_async_copy(src_send.at[0], src_recv.at[0], cr.at[0]).start()

            @pl.when(r == 1)
            def _():
                src_copy(0).start()

    run(lambda i: w_first(i).start(), 1, blocks)

    def w_wait_first(i):
        peer = (me + i) % blocks
        pltpu.make_async_copy(w_recv.at[peer], w_recv.at[peer], w1r.at[peer]).wait()

    run(w_wait_first, 1, blocks)
    reduced = w_recv[0]
    for i in range(1, blocks):
        reduced = reduced + w_recv[i]
    reduced = reduced * grad_scale
    w_sum[...] = reduced[0:padded, :]
    grad_bias[...] = reduced[padded : padded + 1, :]
    w_out[me] = reduced[0:padded, :]
    run(lambda i: w_second(i).start(), 1, blocks)

    total[...] = mm(grad_act[...], self_weight[...], 1, 1)
    for d in range(reach):
        src_wait(d)
        total[...] += src_recv[d].astype(F32)

    @pl.when(c == 1)
    def _():
        src_wait(reach)
        total[...] += src_recv[reach].astype(F32)

    last_send[...] = total[...]
    last = remote(last_send, last_recv, rep_s.at[2], rep_r.at[2], other_rep)
    last.start()

    def w_wait_second(i):
        peer = (me + i) % blocks
        pltpu.make_async_copy(w_out.at[peer], w_out.at[peer], w2r.at[peer]).wait()

    run(w_wait_second, 1, blocks)
    for i in range(blocks):
        which, at = (i * chunk) // width, (i * chunk) % width
        (grad_self, grad_neighbor)[which][at : at + chunk, :] = w_out[i, 0:chunk, :]
    last.wait()
    grad_input[...] = (last_send[...] + last_recv[...]).astype(BF16)

    @pl.when(r == 1)
    def _():
        x_copy(0).wait_send()
        src_copy(0).wait_send()

    for d in range(1, reach):

        @pl.when(x_direct(d))
        def _():
            x_copy(d).wait_send()

        @pl.when(k % 2 == 0)
        def _():
            x_relay(d - 1).wait_send()

        x_pass(d).wait_send()
        src_copy(d).wait_send()

    for d in range(reach - 1):
        pair_copy(d).wait_send()

    @pl.when(c == 0)
    def _():
        x_pass(0).wait_send()
        lone_copy().wait_send()

    @pl.when(c == 1)
    def _():
        x_extra().wait_send()
        pair_copy(reach - 1).wait_send()

    run(lambda i: w_first(i).wait_send(), 1, blocks)
    run(lambda i: w_second(i).wait_send(), 1, blocks)


def finish(*refs):
    for source, target in zip(refs[:5], refs[5:]):
        target[...] = source[...]


def on_device(
    features, tile_values, tile_target, tile_source, tile_count, hub_list, hub_count, hub_weight,
    self_weight, neighbor_weight, bias, cotangent,
):
    blocks = lax.axis_size("blk")
    rows, width = features.shape
    half, slots, tile = tile_values.shape[1:4]
    hubs = hub_list.shape[-1]
    hidden = self_weight.shape[1]
    reach = half // 2
    chunk = 2 * width // blocks
    padded = max(chunk, 8)
    grad_scale = 1.0 / math.sqrt(rows * blocks)
    vmem = pl.BlockSpec(memory_space=pltpu.VMEM)
    smem = pl.BlockSpec(memory_space=pltpu.SMEM)
    dma = pltpu.SemaphoreType.DMA
    V = pltpu.VMEM
    block = (rows, width)
    scratch = [
        V((half, slots, tile, tile), BF16),
        V((half, rows, rows), BF16),
        V((half, rows, rows), BF16),
        V((rows + blocks, width), BF16),
        V((half, rows + blocks, width), BF16),
        V((half, rows, width), BF16),
        V((half * hubs, width), BF16),
        V((half * hubs, rows), BF16),
        V((rows, half * hubs), BF16),
        V(block, F32),
        pltpu.SMEM((half * slots,), jnp.int32),
        V(block, BF16), V(block, BF16),
        V(block, BF16), V(block, BF16),
        V(block, F32), V(block, F32),
        V(block, BF16),
        V((rows, hidden), BF16),
        V((reach,) + block, BF16), V((reach,) + block, BF16),
        V((reach,) + block, BF16), V((reach + 1,) + block, BF16),
        V((blocks, padded + 8, hidden), F32), V((blocks, padded + 8, hidden), F32),
        V((padded, hidden), F32), V((blocks, padded, hidden), F32),
        dma((half,)),
        dma((reach + 1,)), dma((half,)), dma((reach,)), dma((reach,)),
        dma((3,)), dma((3,)),
        dma((reach,)), dma((reach,)),
        dma((reach,)), dma((reach + 1,)),
        dma((blocks,)), dma((blocks,)), dma((blocks,)), dma((blocks,)),
    ]
    out = pl.pallas_call(
        functools.partial(kernel, blocks, grad_scale),
        out_shape=(
            jax.ShapeDtypeStruct((rows, hidden), BF16),
            jax.ShapeDtypeStruct((rows, width), BF16),
            jax.ShapeDtypeStruct((width, hidden), F32),
            jax.ShapeDtypeStruct((width, hidden), F32),
            jax.ShapeDtypeStruct((1, hidden), F32),
        ),
        in_specs=[
            vmem, pl.BlockSpec(memory_space=pl.ANY), smem, smem, smem, vmem, smem, vmem,
            vmem, vmem, vmem, vmem,
        ],
        out_specs=(vmem,) * 5,
        scratch_shapes=scratch,
        compiler_params=pltpu.CompilerParams(
            collective_id=0, has_side_effects=True, vmem_limit_bytes=56 * 1024 * 1024
        ),
    )(
        features, tile_values[0], tile_target[0], tile_source[0], tile_count, hub_list[0],
        hub_count, hub_weight, self_weight, neighbor_weight, bias.reshape(1, hidden), cotangent,
    )
    out = pl.pallas_call(
        finish,
        out_shape=tuple(jax.ShapeDtypeStruct(x.shape, x.dtype) for x in out),
        in_specs=[vmem] * 5,
        out_specs=(vmem,) * 5,
    )(*out)
    return out[0], out[1], out[2], out[3], out[4].reshape(hidden)


def solution(mesh):
    in_specs = (
        P("blk", None),
        P("blk", "rep", None, None, None),
        P("blk", "rep", None),
        P("blk", "rep", None),
        P("blk", "rep"),
        P("blk", None, None),
        P("blk", None),
        P(None, None, "blk"),
        P(None, "rep"),
        P(None, "rep"),
        P("rep"),
        P("blk", "rep"),
    )
    out_specs = (P("blk", "rep"), P("blk", None), P(None, "rep"), P(None, "rep"), P("rep"))
    return jax.shard_map(
        on_device, mesh=mesh, in_specs=in_specs, out_specs=out_specs, check_vma=False
    )
```

```python
import functools
import math

import jax
import jax.numpy as jnp
from jax import lax
from jax.experimental import pallas as pl
from jax.experimental.pallas import tpu as pltpu
from jax.sharding import PartitionSpec as P

MESH = pl.DeviceIdType.MESH
F32 = jnp.float32
BF16 = jnp.bfloat16


def mm(a, b, ca=1, cb=0):
    return lax.dot_general(a, b, (((ca,), (cb,)), ((), ())), preferred_element_type=F32)


def remote(src, dst, send, recv, device):
    return pltpu.make_async_remote_copy(
        src_ref=src, dst_ref=dst, send_sem=send, recv_sem=recv, device_id=device, device_id_type=MESH
    )


def kernel(
    blocks, grad_scale,
    features, tile_values, tile_target, tile_source, tile_count, hub_list, hub_count, hub_weight,
    self_weight, neighbor_weight, bias, cotangent,
    output, grad_input, grad_self, grad_neighbor, grad_bias,
    tiles, dense, dense_t, xsend, xbuf, pick, rows_all, weight_all, weight_t, total, codes,
    part_send, part_recv, back_send, back_recv, last_send, last_recv,
    aggregate, grad_act, pair_send, pair_recv, src_send, src_recv,
    w_send, w_recv, w_sum, w_out,
    tile_sem, xs, xr, fs, rep_s, rep_r, ps, pr, cs, cr, w1s, w1r, w2s, w2r,
):
    half = tile_values.shape[0]
    slots = tile_values.shape[1]
    tile = tile_values.shape[2]
    rows = features.shape[0]
    width = features.shape[1]
    hubs = hub_list.shape[1]
    chips = blocks // 2
    reach = half // 2
    me = lax.axis_index("blk")
    r = lax.axis_index("rep")
    k = me // 2
    c = me % 2
    partner = {"blk": k * 2 + 1 - c}
    other_rep = {"rep": 1 - r}

    for o in range(half):
        pltpu.make_async_copy(tile_values.at[o], tiles.at[o], tile_sem.at[o]).start()
    barrier = pltpu.get_barrier_semaphore()

    def greet(i, carry):
        pl.semaphore_signal(
            barrier, inc=1, device_id={"blk": (me + i) % blocks}, device_id_type=MESH
        )
        return carry

    lax.fori_loop(1, blocks, greet, 0)
    pl.semaphore_signal(barrier, inc=1, device_id=other_rep, device_id_type=MESH)

    xsend[0:rows, :] = features[...]
    reader = lax.broadcasted_iota(jnp.int32, (blocks, hubs), 0)
    slot = lax.broadcasted_iota(jnp.int32, (blocks, hubs), 1)
    counts = jnp.zeros((blocks, hubs), jnp.int32)
    for i in range(blocks):
        counts = jnp.where(reader == i, hub_count[0, i], counts)
    lists = jnp.where(slot < counts, hub_list[...], -1).astype(F32)
    xsend[rows:, :] = jnp.full((blocks, width), -1.0, BF16)
    xsend[rows:, 0:hubs] = lists.astype(BF16)

    pl.semaphore_wait(barrier, blocks)

    def x_copy(d):
        target = ((k + reach * r + d) % chips) * 2 + c
        return remote(xsend, xbuf.at[2 * d], xs.at[d], xr.at[2 * d], {"blk": target})

    def x_extra():
        target = ((k + reach * r + reach) % chips) * 2
        return remote(xsend, xbuf.at[half - 1], xs.at[reach], xr.at[half - 1], {"blk": target})

    def x_pass(d):
        place = 2 * d + 1 - 2 * c
        return remote(xbuf.at[2 * d], xbuf.at[place], fs.at[d], xr.at[place], partner)

    def x_wait(o):
        pltpu.make_async_copy(xbuf.at[o], xbuf.at[o], xr.at[o]).wait()

    @pl.when(r == 0)
    def _():
        pltpu.make_async_copy(xsend, xbuf.at[0], xr.at[0]).start()

    @pl.when(r == 1)
    def _():
        x_copy(0).start()

    for d in range(1, reach):
        x_copy(d).start()

    @pl.when(c == 1)
    def _():
        x_extra().start()

    def code_body(i, carry):
        o, t = i // slots, i % slots
        live = t < tile_count[0, o]
        codes[i] = jnp.where(live, tile_target[o, t] * 2 + tile_source[o, t], -1)
        return carry

    lax.fori_loop(0, half * slots, code_body, 0)

    step = 32

    def build(o, carry):
        pltpu.make_async_copy(tile_values.at[o], tiles.at[o], tile_sem.at[o]).wait()
        for first in range(0, tile, step):
            sums = [jnp.zeros((step, tile), F32) for _ in range(4)]
            for t in range(slots):
                code = codes[o * slots + t]
                value = tiles[o, t, first : first + step, :].astype(F32)
                for q in range(4):
                    sums[q] = sums[q] + value * (code == q).astype(F32)
            for q in range(4):
                i, j = q // 2, q % 2
                dense[o, i * tile + first : i * tile + first + step, j * tile : (j + 1) * tile] = sums[
                    q
                ].astype(BF16)
        dense_t[o] = dense[o].T
        return carry

    for o in range(half):
        source = (me - half * r - o + 2 * blocks) % blocks
        weight_all[o * hubs : (o + 1) * hubs, :] = hub_weight[source]
    weight_t[...] = weight_all[...].T

    for d in range(reach):
        lax.fori_loop(2 * d, 2 * d + 2, build, 0)
        x_wait(2 * d)
        if d == 0:

            @pl.when(c == 0)
            def _():
                x_pass(0).start()

        else:
            x_pass(d).start()

    node = lax.broadcasted_iota(jnp.int32, (rows, width), 0).astype(F32)
    node_lane = lax.broadcasted_iota(jnp.int32, (hubs, rows), 1).astype(F32)
    reader_row = lax.broadcasted_iota(jnp.int32, (blocks, width), 0)
    total[...] = jnp.zeros_like(total)

    def hub_row(o):
        lists = xbuf[o, rows:, :].astype(F32)
        return jnp.sum(jnp.where(reader_row == me, lists, 0.0), axis=0, keepdims=True)

    def forward(o):
        column = jnp.broadcast_to(hub_row(o), (8, width)).T[0:hubs, 0:1]
        chosen = jnp.where(node_lane == column, 1.0, 0.0).astype(BF16)
        block = xbuf[o, 0:rows, :]
        rows_all[o * hubs : (o + 1) * hubs, :] = mm(chosen, block).astype(BF16)
        total[...] += mm(dense[o], block)

    for o in range(0, half, 2):
        forward(o)
    for o in range(1, half, 2):
        x_wait(o)
        forward(o)
    total[...] += mm(weight_t[...], rows_all[...])
    part_send[...] = total[...].astype(BF16)
    part = remote(part_send, part_recv, rep_s.at[0], rep_r.at[0], other_rep)
    part.start()
    own = mm(features[...], self_weight[...]) + bias[...]
    for o in range(half):
        pick[o] = jnp.where(node == hub_row(o), 1.0, 0.0).astype(BF16)
    part.wait()
    aggregate[...] = (total[...] + part_recv[...].astype(F32)).astype(BF16)
    pre = own + mm(aggregate[...], neighbor_weight[...])
    gate = 1.0 / (1.0 + jnp.exp(-pre))
    output[...] = (pre * gate).astype(BF16)
    grad_act[...] = (cotangent[...].astype(F32) * gate * (1.0 + pre * (1.0 - gate))).astype(BF16)
    total[...] = mm(grad_act[...], neighbor_weight[...], 1, 1)
    back_send[...] = total[...].astype(BF16)
    back = remote(back_send, back_recv, rep_s.at[1], rep_r.at[1], other_rep)
    back.start()

    chunk = 2 * width // blocks
    padded = w_out.shape[1]
    sums = (mm(features[...], grad_act[...], 0, 0), mm(aggregate[...], grad_act[...], 0, 0))
    column = jnp.sum(grad_act[...].astype(F32), axis=0, keepdims=True)
    column = jnp.broadcast_to(column, (8, column.shape[1]))
    for i in range(blocks):
        which, at = (i * chunk) // width, (i * chunk) % width
        if padded > chunk:
            w_send[i, 0:padded, :] = jnp.zeros((padded, width), F32)
        w_send[i, 0:chunk, :] = sums[which][at : at + chunk, :]
        w_send[i, padded : padded + 8, :] = column
    w_recv[me] = w_send[me]

    def w_first(i):
        peer = (me + i) % blocks
        return remote(w_send.at[peer], w_recv.at[me], w1s.at[i], w1r.at[me], {"blk": peer})

    def w_second(i):
        peer = (me + i) % blocks
        return remote(w_sum, w_out.at[me], w2s.at[i], w2r.at[me], {"blk": peer})

    def run(body, low, high):
        def wrapped(i, carry):
            body(i)
            return carry

        lax.fori_loop(low, high, wrapped, 0)

    run(lambda i: w_first(i).start(), 1, blocks)
    back.wait()
    grad_aggregate = (total[...] + back_recv[...].astype(F32)).astype(BF16)
    hub_back = mm(weight_all[...], grad_aggregate).astype(BF16)

    def backward(o):
        return mm(dense_t[o], grad_aggregate) + mm(
            pick[o][:, 0:hubs], hub_back[o * hubs : (o + 1) * hubs, :]
        )

    def pair_copy(d):
        place = d + 1 - c
        return remote(pair_send.at[d], pair_recv.at[place], ps.at[d], pr.at[place], partner)

    def lone_copy():
        target = ((k - reach * r - reach + 2 * chips) % chips) * 2 + 1
        return remote(
            pair_send.at[reach - 1], src_recv.at[reach], ps.at[reach - 1], cr.at[reach], {"blk": target}
        )

    def pair_wait(d):
        pltpu.make_async_copy(pair_recv.at[d], pair_recv.at[d], pr.at[d]).wait()

    def src_copy(d):
        target = ((k - reach * r - d + 2 * chips) % chips) * 2 + c
        return remote(src_send.at[d], src_recv.at[d], cs.at[d], cr.at[d], {"blk": target})

    def src_wait(d):
        pltpu.make_async_copy(src_recv.at[d], src_recv.at[d], cr.at[d]).wait()

    for d in range(reach - 1, -1, -1):
        pair_send[d] = backward(2 * d + 1).astype(BF16)
        if d == reach - 1:

            @pl.when(c == 0)
            def _():
                lone_copy().start()

            @pl.when(c == 1)
            def _():
                pair_copy(reach - 1).start()

        else:
            pair_copy(d).start()
    for d in range(reach - 1, -1, -1):
        if d > 0:
            term = backward(2 * d)
            pair_wait(d)
            src_send[d] = (term + pair_recv[d].astype(F32)).astype(BF16)
            src_copy(d).start()
        else:
            total[...] = backward(0)

            @pl.when(c == 0)
            def _():
                pair_wait(0)
                total[...] += pair_recv[0].astype(F32)

            src_send[0] = total[...].astype(BF16)

            @pl.when(r == 0)
            def _():
                pltpu.make_async_copy(src_send.at[0], src_recv.at[0], cr.at[0]).start()

            @pl.when(r == 1)
            def _():
                src_copy(0).start()

    def w_wait_first(i):
        peer = (me + i) % blocks
        pltpu.make_async_copy(w_recv.at[peer], w_recv.at[peer], w1r.at[peer]).wait()

    run(w_wait_first, 1, blocks)
    reduced = w_recv[0]
    for i in range(1, blocks):
        reduced = reduced + w_recv[i]
    reduced = reduced * grad_scale
    w_sum[...] = reduced[0:padded, :]
    grad_bias[...] = reduced[padded : padded + 1, :]
    w_out[me] = reduced[0:padded, :]
    run(lambda i: w_second(i).start(), 1, blocks)

    total[...] = mm(grad_act[...], self_weight[...], 1, 1)
    for d in range(reach):
        src_wait(d)
        total[...] += src_recv[d].astype(F32)

    @pl.when(c == 1)
    def _():
        src_wait(reach)
        total[...] += src_recv[reach].astype(F32)

    last_send[...] = total[...].astype(BF16)
    last = remote(last_send, last_recv, rep_s.at[2], rep_r.at[2], other_rep)
    last.start()

    def w_wait_second(i):
        peer = (me + i) % blocks
        pltpu.make_async_copy(w_out.at[peer], w_out.at[peer], w2r.at[peer]).wait()

    run(w_wait_second, 1, blocks)
    for i in range(blocks):
        which, at = (i * chunk) // width, (i * chunk) % width
        (grad_self, grad_neighbor)[which][at : at + chunk, :] = w_out[i, 0:chunk, :]
    last.wait()
    grad_input[...] = (last_send[...].astype(F32) + last_recv[...].astype(F32)).astype(BF16)

    @pl.when(r == 1)
    def _():
        x_copy(0).wait_send()
        src_copy(0).wait_send()

    for d in range(1, reach):
        x_copy(d).wait_send()
        x_pass(d).wait_send()
        src_copy(d).wait_send()

    for d in range(reach - 1):
        pair_copy(d).wait_send()

    @pl.when(c == 0)
    def _():
        x_pass(0).wait_send()
        lone_copy().wait_send()

    @pl.when(c == 1)
    def _():
        x_extra().wait_send()
        pair_copy(reach - 1).wait_send()

    run(lambda i: w_first(i).wait_send(), 1, blocks)
    run(lambda i: w_second(i).wait_send(), 1, blocks)


def finish(*refs):
    for source, target in zip(refs[:5], refs[5:]):
        target[...] = source[...]


def on_device(
    features, tile_values, tile_target, tile_source, tile_count, hub_list, hub_count, hub_weight,
    self_weight, neighbor_weight, bias, cotangent,
):
    blocks = lax.axis_size("blk")
    rows, width = features.shape
    half, slots, tile = tile_values.shape[1:4]
    hubs = hub_list.shape[-1]
    hidden = self_weight.shape[1]
    reach = half // 2
    chunk = 2 * width // blocks
    padded = max(chunk, 8)
    grad_scale = 1.0 / math.sqrt(rows * blocks)
    vmem = pl.BlockSpec(memory_space=pltpu.VMEM)
    smem = pl.BlockSpec(memory_space=pltpu.SMEM)
    dma = pltpu.SemaphoreType.DMA
    V = pltpu.VMEM
    block = (rows, width)
    scratch = [
        V((half, slots, tile, tile), BF16),
        V((half, rows, rows), BF16),
        V((half, rows, rows), BF16),
        V((rows + blocks, width), BF16),
        V((half, rows + blocks, width), BF16),
        V((half, rows, width), BF16),
        V((half * hubs, width), BF16),
        V((half * hubs, rows), BF16),
        V((rows, half * hubs), BF16),
        V(block, F32),
        pltpu.SMEM((half * slots,), jnp.int32),
        V(block, BF16), V(block, BF16),
        V(block, BF16), V(block, BF16),
        V(block, BF16), V(block, BF16),
        V(block, BF16),
        V((rows, hidden), BF16),
        V((reach,) + block, BF16), V((reach,) + block, BF16),
        V((reach,) + block, BF16), V((reach + 1,) + block, BF16),
        V((blocks, padded + 8, hidden), F32), V((blocks, padded + 8, hidden), F32),
        V((padded, hidden), F32), V((blocks, padded, hidden), F32),
        dma((half,)),
        dma((reach + 1,)), dma((half,)), dma((reach,)),
        dma((3,)), dma((3,)),
        dma((reach,)), dma((reach,)),
        dma((reach,)), dma((reach + 1,)),
        dma((blocks,)), dma((blocks,)), dma((blocks,)), dma((blocks,)),
    ]
    out = pl.pallas_call(
        functools.partial(kernel, blocks, grad_scale),
        out_shape=(
            jax.ShapeDtypeStruct((rows, hidden), BF16),
            jax.ShapeDtypeStruct((rows, width), BF16),
            jax.ShapeDtypeStruct((width, hidden), F32),
            jax.ShapeDtypeStruct((width, hidden), F32),
            jax.ShapeDtypeStruct((1, hidden), F32),
        ),
        in_specs=[
            vmem, pl.BlockSpec(memory_space=pl.ANY), smem, smem, smem, vmem, smem, vmem,
            vmem, vmem, vmem, vmem,
        ],
        out_specs=(vmem,) * 5,
        scratch_shapes=scratch,
        compiler_params=pltpu.CompilerParams(
            collective_id=0, has_side_effects=True, vmem_limit_bytes=56 * 1024 * 1024
        ),
    )(
        features, tile_values[0], tile_target[0], tile_source[0], tile_count, hub_list[0],
        hub_count, hub_weight, self_weight, neighbor_weight, bias.reshape(1, hidden), cotangent,
    )
    out = pl.pallas_call(
        finish,
        out_shape=tuple(jax.ShapeDtypeStruct(x.shape, x.dtype) for x in out),
        in_specs=[vmem] * 5,
        out_specs=(vmem,) * 5,
    )(*out)
    return out[0], out[1], out[2], out[3], out[4].reshape(hidden)


def solution(mesh):
    in_specs = (
        P("blk", None),
        P("blk", "rep", None, None, None),
        P("blk", "rep", None),
        P("blk", "rep", None),
        P("blk", "rep"),
        P("blk", None, None),
        P("blk", None),
        P(None, None, "blk"),
        P(None, "rep"),
        P(None, "rep"),
        P("rep"),
        P("blk", "rep"),
    )
    out_specs = (P("blk", "rep"), P("blk", None), P(None, "rep"), P(None, "rep"), P("rep"))
    return jax.shard_map(
        on_device, mesh=mesh, in_specs=in_specs, out_specs=out_specs, check_vma=False
    )
```
